32 devices in a mesh: light: 16 (over z, y, x), pair: 2 (over core).
Axes of the slice: x: 2, y: 2, z: 4, core: 2. Of those that a mesh axis runs over, the one named last changes fastest.
Arguments:
- tokens: bfloat16 [32768, 2048], P(('light', 'pair')), may hold values from -36 to 36
- norm_gain: float32 [2048], replicated, may hold values from 0.1 to 1.9
- light_gate: bfloat16 [2048, 1280], P(None, 'pair'), may hold values from -0.125 to 0.125
- light_up: bfloat16 [2048, 1280], P(None, 'pair'), may hold values from -0.125 to 0.125
- light_down: bfloat16 [1280, 2048], P('pair'), may hold values from -0.15625 to 0.15625
- heavy_gate: bfloat16 [2048, 10240], P(None, 'light'), may hold values from -0.125 to 0.125
- heavy_up: bfloat16 [2048, 10240], P(None, 'light'), may hold values from -0.125 to 0.125
- heavy_down: bfloat16 [10240, 2048], P('light'), may hold values from -0.0625 to 0.0625
- slot_token_index: int32 [1024], P(('light', 'pair')), may hold values from 0 to 1023, as said below
- slot_active_mask: int32 [1024], P(('light', 'pair')), may hold values from 0 to 1, as said below
Outputs:
- mixed: bfloat16 [32768, 2048], P(('light', 'pair'))
The draws below stay inside these ranges and needn't reach their ends.
Inputs may be any that keep to these rules, and one draw needn't show every extreme that they name: `slot_token_index`: entry s belongs to device s // 32 in the order of light+pair; the live slots of one device name distinct tokens of that device, as positions among its 1024 tokens. `slot_active_mask`: every device has at least one live slot; in every draw some device has all 32 of its slots live.
All inputs are finite; a program needn't handle non-finite values.
Results may differ from the reference program's by a relative error of at most 0.0044.
Values may be sent and summed in bfloat16 or wider, within the bound.
A program may use at most 192 MiB of HBM per device.

```python
import math
import jax
import jax.numpy as jnp
from jax import lax

D = 2048
LF = 1280
HF = 10240
TOK_DEV = 1024
CAP = 32
TOKENS = 32768
N_LIGHT = 16
N_PAIR = 2


def routing_tables(key):
    first_key, second_key, third_key, fourth_key, fifth_key = jax.random.split(jax.random.fold_in(key, 7), 5)
    devices_all = N_LIGHT * N_PAIR
    left_draw = jax.random.randint(first_key, (devices_all,), 0, CAP + 1)
    right_draw = jax.random.randint(second_key, (devices_all,), 0, CAP + 1)
    routed_counts = jnp.minimum(CAP // 2 + left_draw * right_draw // (2 * CAP), CAP)
    routed_counts = jnp.maximum(routed_counts, 1)
    busiest = jax.random.randint(third_key, (), 0, devices_all)
    routed_counts = jnp.where(jnp.arange(devices_all) == busiest, CAP, routed_counts)
    token_keys = jax.random.split(fourth_key, devices_all)
    selected_tokens = jax.vmap(lambda sub_key: jax.random.permutation(sub_key, TOK_DEV)[:CAP])(token_keys)
    rank_keys = jax.random.split(fifth_key, devices_all)
    router_scores = jax.vmap(lambda sub_key: jax.random.permutation(sub_key, CAP))(rank_keys)
    active_flags = (router_scores < routed_counts[:, None]).astype(jnp.int32)
    return (selected_tokens.reshape(-1).astype(jnp.int32), active_flags.reshape(-1))


def draw_slot_token_index(key, part):
    return routing_tables(key)[0]


def draw_slot_active_mask(key, part):
    return routing_tables(key)[1]


def draw_tokens(key, part):
    first_key, second_key, third_key = jax.random.split(jax.random.fold_in(key, 11), 3)
    row_scale = jnp.exp(jax.random.uniform(first_key, (TOKENS, 1), jnp.float32, math.log(0.3), math.log(3.0)))
    column_scale = jnp.exp(jax.random.uniform(second_key, (1, D), jnp.float32, math.log(0.3), math.log(3.0)))
    base = jnp.clip(jax.random.normal(third_key, (TOKENS, D), jnp.float32), -4.0, 4.0)
    return (base * row_scale * column_scale).astype(jnp.bfloat16)


def levels(stream_key, dims, cuts, least, high):
    def one(position, parts):
        steps = jax.random.uniform(jax.random.fold_in(jax.random.fold_in(stream_key, 6), position), (parts,), jnp.float32, least / len(cuts), high / len(cuts))
        return jnp.repeat(jnp.exp(steps), dims[position] // parts).reshape((-1,) + (1,) * (len(dims) - position - 1))

    gain = one(*cuts[0])
    for cut in cuts[1:]:
        gain = gain * one(*cut)
    return gain


def noise(rng, extent, deviation, reach, cuts=(), kind=jnp.bfloat16):
    drawn = deviation * jax.random.normal(rng, extent, jnp.float32)
    if cuts:
        drawn = drawn * levels(rng, extent, cuts, -0.22, 0.18)
    return jnp.clip(drawn, -reach, reach).astype(kind)


def setup_inputs(seed: int = 0) -> dict:
    seeds = jax.random.split(jax.random.key(seed), 11)
    tokens = draw_tokens(jax.random.fold_in(seeds[10], 71), 0)
    norm_gain = jnp.clip(1.0 + 0.18 * jax.random.normal(seeds[1], (D,), jnp.float32), 0.1, 1.9)
    light_gate = noise(seeds[2], (D, LF), D ** -0.5, 0.125, ((1, 2),))
    light_up = noise(seeds[3], (D, LF), D ** -0.5, 0.125, ((1, 2),))
    light_down = noise(seeds[4], (LF, D), LF ** -0.5, 0.15625, ((0, 2),))
    heavy_gate = noise(seeds[5], (D, HF), D ** -0.5, 0.125, ((1, 16),))
    heavy_up = noise(seeds[6], (D, HF), D ** -0.5, 0.125, ((1, 16),))
    heavy_down = noise(seeds[7], (HF, D), HF ** -0.5, 0.0625, ((0, 16),))
    slot_token_index = draw_slot_token_index(jax.random.fold_in(seeds[10], 71), 0)
    slot_active_mask = draw_slot_active_mask(jax.random.fold_in(seeds[10], 71), 0)
    return dict(tokens=tokens, norm_gain=norm_gain, light_gate=light_gate, light_up=light_up, light_down=light_down, heavy_gate=heavy_gate, heavy_up=heavy_up, heavy_down=heavy_down, slot_token_index=slot_token_index, slot_active_mask=slot_active_mask)


epsilon = 1e-06

def gated_units(rows, w_gate, w_up):
    gate = jnp.dot(rows, w_gate, preferred_element_type=jnp.float32)
    upward = jnp.dot(rows, w_up, preferred_element_type=jnp.float32)
    return (jax.nn.silu(gate) * upward).astype(jnp.bfloat16)

def reference(tokens, norm_gain, light_gate, light_up, light_down, heavy_gate, heavy_up, heavy_down, slot_token_index, slot_active_mask):
    residual = tokens.astype(jnp.float32)
    mean_square = lax.optimization_barrier(jnp.mean(residual * residual, axis=-1, keepdims=True))
    normalized_input = (residual * lax.rsqrt(mean_square + epsilon) * norm_gain.astype(jnp.float32)).astype(jnp.bfloat16)
    light_hidden = gated_units(normalized_input, light_gate, light_up)
    light_out = jnp.dot(light_hidden, light_down, preferred_element_type=jnp.float32)
    owning = (jnp.arange(CAP * N_LIGHT * N_PAIR, dtype=jnp.int32) // CAP).astype(jnp.int32)
    global_token_index = (owning * TOK_DEV + slot_token_index).astype(jnp.int32)
    active_flags = slot_active_mask.astype(jnp.bfloat16)[:, None]
    routed_output = normalized_input[global_token_index] * active_flags
    heavy_hidden = gated_units(routed_output, heavy_gate, heavy_up)
    heavy_out = jnp.dot(heavy_hidden, heavy_down, preferred_element_type=jnp.float32)
    weighted = heavy_out * slot_active_mask.astype(jnp.float32)[:, None]
    routed_sum = jnp.zeros((TOKENS, D), jnp.float32).at[global_token_index].add(weighted)
    return (residual + light_out + routed_sum).astype(jnp.bfloat16)
```

```python
import functools

import jax
import jax.numpy as jnp
from jax import lax
from jax.experimental import pallas as pl
from jax.experimental.pallas import tpu as pltpu
from jax.sharding import PartitionSpec as P

epsilon = 1e-06
MESH = pl.DeviceIdType.MESH
F32, BF16 = jnp.float32, jnp.bfloat16
ORDERS = ((0, 1, 2), (0, 2, 1))


def three_factors(n):
    dims, left = [], n
    for power in (3, 2, 1):
        f = 1
        while f**power < left or left % f:
            f += 1
        dims.append(f)
        left //= f
    return tuple(dims)


def kth_nearest(k, x, length):
    if k == 0:
        return x
    if length == 2:
        return 1 - x
    reach = jnp.minimum(x, length - 1 - x)
    sign = jnp.where(2 * x < length, 1, -1)
    both = k <= 2 * reach
    distance = jnp.where(both, (k + 1) // 2, k - reach)
    return x + distance * jnp.where(both, sign * (1 if k % 2 else -1), sign)


class Plan:
    def __init__(self, dims, me):
        self.dims = dims
        a, b, c = dims
        self.my = (me // (b * c), me // c % b, me % c)
        self.slots = []
        self.base = []
        for order in ORDERS:
            base, total, before = [], 0, 1
            for dim in order:
                base.append(total)
                length = dims[dim]
                total += before if length == 2 else before * (length + 1)
                before *= length
            self.base.append(base)
            self.slots.append(total)

    def events(self, h):
        a, p, q = (self.dims[d] for d in ORDERS[h])
        every = [(i, j, k) for i in range(a) for j in range(p) for k in range(q)]
        every.sort(key=lambda e: (e[2], e[0] + e[1], e[1]))
        return every[1:]

    def token(self, h, e):
        t = [None] * 3
        for lvl, dim in enumerate(ORDERS[h]):
            t[dim] = kth_nearest(e[lvl], self.my[dim], self.dims[dim])
        return tuple(t)

    def index(self, t):
        return (t[0] * self.dims[1] + t[1]) * self.dims[2] + t[2]

    def place(self, t, at):
        a, b, c = self.dims
        group = (t[1] - at[1] + b) % b * c + (t[2] - at[2] + c) % c
        return (group + b * c - 1) % (b * c) * a + t[0]

    def top(self, e):
        return max([-1] + [lvl for lvl in range(3) if e[lvl]])

    def moved(self, dim, x):
        at = list(self.my)
        at[dim] = x
        return tuple(at)

    def children(self, h, e):
        t, top, out = self.token(h, e), self.top(e), []
        for lvl in range(max(top, 0), 3):
            dim = ORDERS[h][lvl]
            length, x = self.dims[dim], self.my[dim]
            if length == 1:
                continue
            if lvl == top:
                if length > 2:
                    to = x + jnp.where(t[dim] < x, 1, -1)
                    cond = (to >= 0) & (to < length)
                    out.append((self.moved(dim, to), cond, self.slot(h, lvl, t, False)))
            elif length == 2:
                out.append((self.moved(dim, 1 - x), None, self.slot(h, lvl, t, False)))
            else:
                out.append((self.moved(dim, x + 1), x < length - 1, self.slot(h, lvl, t, False)))
                out.append((self.moved(dim, x - 1), x > 0, self.slot(h, lvl, t, True)))
        return out

    def slot(self, h, lvl, t, extra):
        order = ORDERS[h]
        prefix, before = 0, 1
        for dim in order[:lvl]:
            prefix = prefix * self.dims[dim] + t[dim]
            before *= self.dims[dim]
        length = self.dims[order[lvl]]
        base = self.base[h][lvl]
        if length == 2:
            return base + prefix
        main = base + prefix * length + t[order[lvl]]
        other = base + before * length + prefix
        if isinstance(extra, bool):
            return other if extra else main
        return jnp.where(extra, other, main)

    def parent(self, h, e):
        t, lvl = self.token(h, e), self.top(e)
        dim = ORDERS[h][lvl]
        x = self.my[dim]
        to = 1 - x if self.dims[dim] == 2 else x + jnp.where(t[dim] > x, 1, -1)
        extra = False if self.dims[dim] == 2 else (to == t[dim]) & (x < to)
        return self.moved(dim, to), self.slot(h, lvl, t, extra)


def when(cond, act):
    if cond is None:
        act()
    else:
        pl.when(cond)(act)


def normalize(rows, gain):
    square = jnp.mean(rows * rows, axis=-1, keepdims=True)
    return (rows * lax.rsqrt(square + epsilon) * gain).astype(BF16)


def gated_tile(x, gate, up):
    width = gate.shape[1]
    both = jnp.dot(x, jnp.concatenate([gate, up], axis=1), preferred_element_type=F32)
    g, u = both[:, :width], both[:, width:]
    return (g / (1.0 + jnp.exp(-g)) * u).astype(BF16)


def gated(x_ref, rows, gate_ref, up_ref, out_ref, out_rows, offset):
    width = gate_ref.shape[-1]
    if width % 128:
        x = x_ref[rows, :]
        g = jnp.dot(x, gate_ref[...], preferred_element_type=F32)
        u = jnp.dot(x, up_ref[...], preferred_element_type=F32)
        out_ref[out_rows, offset : offset + width] = (g / (1.0 + jnp.exp(-g)) * u).astype(BF16)
        return

    @pl.loop(0, width // 128)
    def _(j):
        cols = pl.ds(pl.multiple_of(j * 128, 128), 128)
        to = pl.ds(pl.multiple_of(offset + j * 128, 128), 128)
        out_ref[out_rows, to] = gated_tile(x_ref[rows, :], gate_ref[:, cols], up_ref[:, cols])


def routed_kernel(
    n, dims, *refs
):
    (tok_hbm, gain, lg_hbm, lu_hbm, ld_hbm, hg_hbm, hu_hbm, hd_hbm, idx, mask) = refs[:10]
    (base_hbm, heavy_ref) = refs[10:12]
    (tok, normed, lg, lu, ld, hg, hu, hd, hidden, hhidden, picked, rows_in, rows_out, back) = refs[12:26]
    (load_sem, pair_send, pair_recv, store_sem, g_send, g_recv, s_send, s_recv) = refs[26:]
    count, width = tok.shape
    cap = picked.shape[0]
    half = width // 2
    part = lg.shape[2]
    me, core = lax.axis_index("light"), lax.axis_index("pair")
    plan = Plan(dims, me)
    chunk = 256

    loads = [
        pltpu.make_async_copy(s, d, load_sem.at[i])
        for i, (s, d) in enumerate(
            [
                (tok_hbm, tok),
                (lg_hbm, lg.at[0]),
                (lu_hbm, lu.at[0]),
                (hg_hbm, hg),
                (hu_hbm, hu),
                (hd_hbm, hd),
                (ld_hbm, ld.at[0:part]),
            ]
        )
    ]
    for copy in loads:
        copy.start()

    barrier = pltpu.get_barrier_semaphore()
    neighbours = [({"pair": 1 - core}, None)]
    for dim, length in enumerate(dims):
        x = plan.my[dim]
        if length == 2:
            neighbours.append(({"light": plan.index(plan.moved(dim, 1 - x))}, None))
        elif length > 2:
            neighbours.append(({"light": plan.index(plan.moved(dim, x + 1))}, x < length - 1))
            neighbours.append(({"light": plan.index(plan.moved(dim, x - 1))}, x > 0))
    total = 0
    for device, cond in neighbours:
        when(
            cond,
            lambda device=device: pl.semaphore_signal(
                barrier, inc=1, device_id=device, device_id_type=MESH
            ),
        )
        total = total + (1 if cond is None else jnp.where(cond, 1, 0))
    pl.semaphore_wait(barrier, total)

    swaps = [
        pltpu.make_async_remote_copy(
            src_ref=s,
            dst_ref=d,
            send_sem=pair_send.at[i],
            recv_sem=pair_recv.at[i],
            device_id={"pair": 1 - core},
            device_id_type=MESH,
        )
        for i, (s, d) in enumerate(
            [(lg_hbm, lg.at[1]), (lu_hbm, lu.at[1]), (ld_hbm, ld.at[part : 2 * part])]
        )
    ]

    loads[0].wait()

    row_id = lax.broadcasted_iota(jnp.int32, (cap, count), 1)
    taking = jnp.where((row_id == idx[...]) & (mask[...] == 1), 1.0, 0.0).astype(BF16)
    for j in range(width // 512):
        cols = slice(j * 512, (j + 1) * 512)
        picked[:, cols] = jnp.dot(taking, tok[:, cols], preferred_element_type=F32)

    def rows_of(t):
        return pl.ds(pl.multiple_of(plan.place(t, plan.my) * cap, cap), cap)

    mine = rows_of(plan.my)
    rows_in[mine, :] = normalize(picked[...], gain[...])

    sends = []

    def spread(h, e):
        t = plan.token(h, e)
        cols = pl.ds(h * half, half)
        for to, cond, _ in plan.children(h, e):
            target = pl.ds(pl.multiple_of(plan.place(t, to) * cap, cap), cap)
            copy = pltpu.make_async_remote_copy(
                src_ref=rows_in.at[rows_of(t), cols],
                dst_ref=rows_in.at[target, cols],
                send_sem=g_send.at[len(sends)],
                recv_sem=g_recv.at[h, plan.index(t)],
                device_id={"light": plan.index(to)},
                device_id_type=MESH,
            )
            when(cond, copy.start)
            sends.append((copy, cond))

    def arrive(h, e):
        t = plan.token(h, e)
        view = rows_in.at[rows_of(t), pl.ds(h * half, half)]
        pltpu.make_async_copy(view, view, g_recv.at[h, plan.index(t)]).wait()

    own = (0, 0, 0)
    for h in range(2):
        spread(h, own)
    for copy in swaps:
        copy.start()

    def norm_piece(i):
        @pl.loop(0, chunk // 32)
        def _(r):
            rows = pl.ds(pl.multiple_of(i * chunk + r * 32, 32), 32)
            normed[rows, :] = normalize(tok[rows, :].astype(F32), gain[...])

    def gated_piece(i, side):
        if i == 0:
            if side == 0:
                loads[1].wait()
                loads[2].wait()
            else:
                swaps[0].wait_recv()
                swaps[1].wait_recv()
        rows = pl.ds(i * chunk, chunk)
        gated(normed, rows, lg.at[side], lu.at[side], hidden, rows, side * part)

    stores = []

    def down_piece(i):
        if i == 0:
            loads[6].wait()
            swaps[2].wait_recv()
        rows = pl.ds(i * chunk, chunk)

        @pl.loop(0, width // 256)
        def _(j):
            cols = pl.ds(pl.multiple_of(j * 256, 256), 256)
            out = jnp.dot(hidden[rows, :], ld[:, cols], preferred_element_type=F32)
            tok[rows, cols] = (tok[rows, cols].astype(F32) + out).astype(BF16)

        copy = pltpu.make_async_copy(tok.at[rows], base_hbm.at[rows], store_sem.at[i])
        copy.start()
        stores.append(copy)

    chunks = count // chunk
    before = []
    for i in range(chunks):
        before += [functools.partial(norm_piece, i), functools.partial(gated_piece, i, 0)]
    after = [functools.partial(gated_piece, i, 1) for i in range(chunks)]
    after += [functools.partial(down_piece, i) for i in range(chunks)]

    events = [plan.events(h) for h in range(2)]
    inners = [[e for e in events[h] if e[2] == 0] for h in range(2)]
    outers = [[e for e in events[h] if e[2]] for h in range(2)]

    steps = max(len(x) for x in inners)
    for s in range(max(steps, len(before))):
        if s < len(before):
            before[s]()
        for h in range(2):
            if s < len(inners[h]):
                arrive(h, inners[h][s])
                spread(h, inners[h][s])

    blocks = n * cap
    size = min(chunk, blocks)
    parts = blocks // size
    known = dims[1] <= 2 and dims[2] <= 2

    def part_of(h, e):
        if not known:
            return None
        rel = [0, 0, 0]
        for lvl, dim in enumerate(ORDERS[h]):
            rel[dim] = e[lvl]
        groups = dims[1] * dims[2]
        rank = (rel[1] * dims[2] + rel[2] + groups - 1) % groups
        return rank * dims[0] * cap // size

    def heavy_part(k):
        if k == 0:
            loads[3].wait()
            loads[4].wait()
            loads[5].wait()
        rows = pl.ds(k * size, size)
        gated(rows_in, rows, hg, hu, hhidden, pl.ds(0, size), 0)

        @pl.loop(0, width // 256)
        def _(j):
            cols = pl.ds(pl.multiple_of(j * 256, 256), 256)
            out = jnp.dot(hhidden[...], hd[:, cols], preferred_element_type=F32)
            rows_out[rows, cols] = out.astype(BF16)

    returns = []

    def collect(h, e):
        t = plan.token(h, e)
        rows, cols = rows_of(t), pl.ds(h * half, half)
        for _, cond, slot in plan.children(h, e):

            def take(slot=slot):
                view = back.at[h, slot]
                pltpu.make_async_copy(view, view, s_recv.at[h, slot]).wait()
                added = rows_out[rows, cols].astype(F32) + view[...].astype(F32)
                rows_out[rows, cols] = added.astype(BF16)

            when(cond, take)
        if plan.top(e) < 0:
            heavy_ref[:, cols] = rows_out[rows, cols]
            return
        to, slot = plan.parent(h, e)
        copy = pltpu.make_async_remote_copy(
            src_ref=rows_out.at[rows, cols],
            dst_ref=back.at[h, slot],
            send_sem=s_send.at[len(returns)],
            recv_sem=s_recv.at[h, slot],
            device_id={"light": plan.index(to)},
            device_id_type=MESH,
        )
        copy.start()
        returns.append(copy)

    arrived, returned = set(), set()
    for k in range(parts):
        for s in range(max(len(x) for x in outers)):
            for h in range(2):
                if s < len(outers[h]) and (h, outers[h][s]) not in arrived:
                    e = outers[h][s]
                    if part_of(h, e) in (None, k):
                        arrived.add((h, e))
                        arrive(h, e)
                        spread(h, e)
        heavy_part(k)
        if k == parts - 1 or known:
            for s in range(max(len(x) for x in outers)):
                for h in range(2):
                    if s < len(outers[h]):
                        e = outers[h][-1 - s]
                        if (h, e) not in returned and (k == parts - 1 or part_of(h, e) == k):
                            returned.add((h, e))
                            collect(h, e)

    for s in range(max(steps, len(after))):
        if s < len(after):
            after[s]()
        for h in range(2):
            if s < len(inners[h]):
                collect(h, inners[h][-1 - s])
    for h in range(2):
        collect(h, own)

    for copy, cond in sends:
        when(cond, copy.wait_send)
    for copy in returns:
        copy.wait_send()
    for copy in swaps:
        copy.wait_send()
    for copy in stores:
        copy.wait()


def place_kernel(base, heavy, idx, mask, out):
    rows, cap = base.shape[0], idx.shape[1]
    row_id = lax.broadcasted_iota(jnp.int32, (rows, cap), 0) + pl.program_id(0) * rows
    placing = jnp.where((row_id == idx[...]) & (mask[...] == 1), 1.0, 0.0).astype(BF16)
    added = jnp.dot(placing, heavy[...], preferred_element_type=F32)
    out[...] = (base[...].astype(F32) + added).astype(BF16)


def edge_counts(dims):
    plan = Plan(dims, 0)
    return [
        sum(len(plan.children(h, e)) for e in [(0, 0, 0)] + plan.events(h)) for h in range(2)
    ], plan.slots


def body(
    n,
    tokens,
    norm_gain,
    light_gate,
    light_up,
    light_down,
    heavy_gate,
    heavy_up,
    heavy_down,
    slot_token_index,
    slot_active_mask,
):
    count, width = tokens.shape
    cap = slot_token_index.shape[0]
    part, heavy = light_gate.shape[1], heavy_gate.shape[1]
    dims = three_factors(n)
    edges, slots = edge_counts(dims)
    blocks = n * cap
    hbm = pl.BlockSpec(memory_space=pl.ANY)
    vmem = pl.BlockSpec(memory_space=pltpu.VMEM)
    dma = pltpu.SemaphoreType.DMA
    base, rows = pl.pallas_call(
        functools.partial(routed_kernel, n, dims),
        out_shape=(
            jax.ShapeDtypeStruct((count, width), BF16),
            jax.ShapeDtypeStruct((cap, width), BF16),
        ),
        in_specs=[hbm, vmem] + [hbm] * 6 + [vmem] * 2,
        out_specs=(hbm, vmem),
        scratch_shapes=[
            pltpu.VMEM((count, width), BF16),
            pltpu.VMEM((count, width), BF16),
            pltpu.VMEM((2, width, part), BF16),
            pltpu.VMEM((2, width, part), BF16),
            pltpu.VMEM((2 * part, width), BF16),
            pltpu.VMEM((width, heavy), BF16),
            pltpu.VMEM((width, heavy), BF16),
            pltpu.VMEM((heavy, width), BF16),
            pltpu.VMEM((count, 2 * part), BF16),
            pltpu.VMEM((min(256, blocks), heavy), BF16),
            pltpu.VMEM((cap, width), F32),
            pltpu.VMEM((blocks, width), BF16),
            pltpu.VMEM((blocks, width), BF16),
            pltpu.VMEM((2, max(slots), cap, width // 2), BF16),
            dma((7,)),
            dma((3,)),
            dma((3,)),
            dma((count // 256,)),
            dma((sum(edges),)),
            dma((2, n)),
            dma((2 * (n - 1),)),
            dma((2, max(slots))),
        ],
        compiler_params=pltpu.CompilerParams(
            collective_id=0, has_side_effects=True, vmem_limit_bytes=62 * 2**20
        ),
    )(
        tokens,
        norm_gain.astype(F32)[None, :],
        light_gate,
        light_up,
        light_down,
        heavy_gate,
        heavy_up,
        heavy_down,
        slot_token_index[:, None],
        slot_active_mask[:, None],
    )
    tile = 256
    return pl.pallas_call(
        place_kernel,
        grid=(count // tile,),
        out_shape=jax.ShapeDtypeStruct((count, width), BF16),
        in_specs=[
            pl.BlockSpec((tile, width), lambda i: (i, 0)),
            pl.BlockSpec((cap, width), lambda i: (0, 0)),
            pl.BlockSpec((1, cap), lambda i: (0, 0)),
            pl.BlockSpec((1, cap), lambda i: (0, 0)),
        ],
        out_specs=pl.BlockSpec((tile, width), lambda i: (i, 0)),
    )(base, rows, slot_token_index[None, :], slot_active_mask[None, :])


def solution(mesh):
    placed = (
        P(("light", "pair"), None),
        P(),
        P(None, "pair"),
        P(None, "pair"),
        P("pair", None),
        P(None, "light"),
        P(None, "light"),
        P("light", None),
        P(("light", "pair")),
        P(("light", "pair")),
    )
    return jax.shard_map(
        functools.partial(body, mesh.shape["light"]),
        mesh=mesh,
        in_specs=placed,
        out_specs=P(("light", "pair"), None),
        check_vma=False,
    )
```

```python
import functools

import jax
import jax.numpy as jnp
from jax import lax
from jax.experimental import pallas as pl
from jax.experimental.pallas import tpu as pltpu
from jax.sharding import PartitionSpec as P

epsilon = 1e-06
MESH = pl.DeviceIdType.MESH
F32, BF16 = jnp.float32, jnp.bfloat16
ORDERS = ((0, 1, 2), (0, 2, 1))


def three_factors(n):
    dims, left = [], n
    for power in (3, 2, 1):
        f = 1
        while f**power < left or left % f:
            f += 1
        dims.append(f)
        left //= f
    return tuple(dims)


def kth_nearest(k, x, length):
    if k == 0:
        return x
    if length == 2:
        return 1 - x
    reach = jnp.minimum(x, length - 1 - x)
    sign = jnp.where(2 * x < length, 1, -1)
    both = k <= 2 * reach
    distance = jnp.where(both, (k + 1) // 2, k - reach)
    return x + distance * jnp.where(both, sign * (1 if k % 2 else -1), sign)


class Plan:
    def __init__(self, dims, me):
        self.dims = dims
        a, b, c = dims
        self.my = (me // (b * c), me // c % b, me % c)
        self.slots = []
        self.base = []
        for order in ORDERS:
            base, total, before = [], 0, 1
            for dim in order:
                base.append(total)
                length = dims[dim]
                total += before if length == 2 else before * (length + 1)
                before *= length
            self.base.append(base)
            self.slots.append(total)

    def events(self, h):
        a, p, q = (self.dims[d] for d in ORDERS[h])
        every = [(i, j, k) for i in range(a) for j in range(p) for k in range(q)]
        every.sort(key=lambda e: (e[2], e[0] + e[1], e[1]))
        return every[1:]

    def token(self, h, e):
        t = [None] * 3
        for lvl, dim in enumerate(ORDERS[h]):
            t[dim] = kth_nearest(e[lvl], self.my[dim], self.dims[dim])
        return tuple(t)

    def index(self, t):
        return (t[0] * self.dims[1] + t[1]) * self.dims[2] + t[2]

    def place(self, t, at):
        a, b, c = self.dims
        group = (t[1] - at[1] + b) % b * c + (t[2] - at[2] + c) % c
        return (group + b * c - 1) % (b * c) * a + t[0]

    def top(self, e):
        return max([-1] + [lvl for lvl in range(3) if e[lvl]])

    def moved(self, dim, x):
        at = list(self.my)
        at[dim] = x
        return tuple(at)

    def children(self, h, e):
        t, top, out = self.token(h, e), self.top(e), []
        for lvl in range(max(top, 0), 3):
            dim = ORDERS[h][lvl]
            length, x = self.dims[dim], self.my[dim]
            if length == 1:
                continue
            if lvl == top:
                if length > 2:
                    to = x + jnp.where(t[dim] < x, 1, -1)
                    cond = (to >= 0) & (to < length)
                    out.append((self.moved(dim, to), cond, self.slot(h, lvl, t, False)))
            elif length == 2:
                out.append((self.moved(dim, 1 - x), None, self.slot(h, lvl, t, False)))
            else:
                out.append((self.moved(dim, x + 1), x < length - 1, self.slot(h, lvl, t, False)))
                out.append((self.moved(dim, x - 1), x > 0, self.slot(h, lvl, t, True)))
        return out

    def slot(self, h, lvl, t, extra):
        order = ORDERS[h]
        prefix, before = 0, 1
        for dim in order[:lvl]:
            prefix = prefix * self.dims[dim] + t[dim]
            before *= self.dims[dim]
        length = self.dims[order[lvl]]
        base = self.base[h][lvl]
        if length == 2:
            return base + prefix
        main = base + prefix * length + t[order[lvl]]
        other = base + before * length + prefix
        if isinstance(extra, bool):
            return other if extra else main
        return jnp.where(extra, other, main)

    def parent(self, h, e):
        t, lvl = self.token(h, e), self.top(e)
        dim = ORDERS[h][lvl]
        x = self.my[dim]
        to = 1 - x if self.dims[dim] == 2 else x + jnp.where(t[dim] > x, 1, -1)
        extra = False if self.dims[dim] == 2 else (to == t[dim]) & (x < to)
        return self.moved(dim, to), self.slot(h, lvl, t, extra)


def when(cond, act):
    if cond is None:
        act()
    else:
        pl.when(cond)(act)


def normalize(rows, gain):
    square = jnp.mean(rows * rows, axis=-1, keepdims=True)
    return (rows * lax.rsqrt(square + epsilon) * gain).astype(BF16)


def gated_tile(x, gate, up):
    width = gate.shape[1]
    both = jnp.dot(x, jnp.concatenate([gate, up], axis=1), preferred_element_type=F32)
    g, u = both[:, :width], both[:, width:]
    return (g / (1.0 + jnp.exp(-g)) * u).astype(BF16)


def gated(x_ref, rows, gate_ref, up_ref, out_ref, out_rows, offset):
    width = gate_ref.shape[-1]
    if width % 128:
        x = x_ref[rows, :]
        g = jnp.dot(x, gate_ref[...], preferred_element_type=F32)
        u = jnp.dot(x, up_ref[...], preferred_element_type=F32)
        out_ref[out_rows, offset : offset + width] = (g / (1.0 + jnp.exp(-g)) * u).astype(BF16)
        return

    @pl.loop(0, width // 128)
    def _(j):
        cols = pl.ds(pl.multiple_of(j * 128, 128), 128)
        to = pl.ds(pl.multiple_of(offset + j * 128, 128), 128)
        out_ref[out_rows, to] = gated_tile(x_ref[rows, :], gate_ref[:, cols], up_ref[:, cols])


def routed_kernel(
    n, dims, *refs
):
    (tok_hbm, gain, lg_hbm, lu_hbm, ld_hbm, hg_hbm, hu_hbm, hd_hbm, idx, mask) = refs[:10]
    (base_hbm, heavy_ref) = refs[10:12]
    (tok, normed, lg, lu, ld, hg, hu, hd, hidden, hhidden, picked, rows_in, rows_out, back) = refs[12:26]
    (load_sem, pair_send, pair_recv, store_sem, g_send, g_recv, s_send, s_recv) = refs[26:]
    count, width = tok.shape
    cap = picked.shape[0]
    half = width // 2
    part = lg.shape[2]
    me, core = lax.axis_index("light"), lax.axis_index("pair")
    plan = Plan(dims, me)
    chunk = 256

    loads = [
        pltpu.make_async_copy(s, d, load_sem.at[i])
        for i, (s, d) in enumerate(
            [
                (tok_hbm, tok),
                (lg_hbm, lg.at[0]),
                (lu_hbm, lu.at[0]),
                (hg_hbm, hg),
                (hu_hbm, hu),
                (hd_hbm, hd),
                (ld_hbm, ld.at[0:part]),
            ]
        )
    ]
    loads[0].start()

    barrier = pltpu.get_barrier_semaphore()
    neighbours = [({"pair": 1 - core}, None)]
    for dim, length in enumerate(dims):
        x = plan.my[dim]
        if length == 2:
            neighbours.append(({"light": plan.index(plan.moved(dim, 1 - x))}, None))
        elif length > 2:
            neighbours.append(({"light": plan.index(plan.moved(dim, x + 1))}, x < length - 1))
            neighbours.append(({"light": plan.index(plan.moved(dim, x - 1))}, x > 0))
    total = 0
    for device, cond in neighbours:
        when(
            cond,
            lambda device=device: pl.semaphore_signal(
                barrier, inc=1, device_id=device, device_id_type=MESH
            ),
        )
        total = total + (1 if cond is None else jnp.where(cond, 1, 0))
    pl.semaphore_wait(barrier, total)

    swaps = [
        pltpu.make_async_remote_copy(
            src_ref=s,
            dst_ref=d,
            send_sem=pair_send.at[i],
            recv_sem=pair_recv.at[i],
            device_id={"pair": 1 - core},
            device_id_type=MESH,
        )
        for i, (s, d) in enumerate(
            [(lg_hbm, lg.at[1]), (lu_hbm, lu.at[1]), (ld_hbm, ld.at[part : 2 * part])]
        )
    ]

    loads[0].wait()
    for copy in loads[1:]:
        copy.start()

    live = jnp.where(mask[...] == 1, idx[...], -1).astype(F32)
    diagonal = lax.broadcasted_iota(jnp.int32, (cap, cap), 0) == lax.broadcasted_iota(
        jnp.int32, (cap, cap), 1
    )
    wanted = jnp.sum(jnp.where(diagonal, live, 0.0), axis=1, keepdims=True)
    row_id = lax.broadcasted_iota(jnp.int32, (cap, count), 1).astype(F32)
    taking = jnp.where(row_id == wanted, 1.0, 0.0).astype(BF16)
    for j in range(width // 512):
        cols = slice(j * 512, (j + 1) * 512)
        picked[:, cols] = jnp.dot(taking, tok[:, cols], preferred_element_type=F32)

    def rows_of(t):
        return pl.ds(pl.multiple_of(plan.place(t, plan.my) * cap, cap), cap)

    mine = rows_of(plan.my)
    rows_in[mine, :] = normalize(picked[...], gain[...])

    sends = []

    def spread(h, e):
        t = plan.token(h, e)
        cols = pl.ds(h * half, half)
        for to, cond, _ in plan.children(h, e):
            target = pl.ds(pl.multiple_of(plan.place(t, to) * cap, cap), cap)
            copy = pltpu.make_async_remote_copy(
                src_ref=rows_in.at[rows_of(t), cols],
                dst_ref=rows_in.at[target, cols],
                send_sem=g_send.at[len(sends)],
                recv_sem=g_recv.at[h, plan.index(t)],
                device_id={"light": plan.index(to)},
                device_id_type=MESH,
            )
            when(cond, copy.start)
            sends.append((copy, cond))

    def arrive(h, e):
        t = plan.token(h, e)
        view = rows_in.at[rows_of(t), pl.ds(h * half, half)]
        pltpu.make_async_copy(view, view, g_recv.at[h, plan.index(t)]).wait()

    own = (0, 0, 0)
    for h in range(2):
        spread(h, own)
    for copy in swaps:
        copy.start()

    def norm_piece(i):
        @pl.loop(0, chunk // 32)
        def _(r):
            rows = pl.ds(pl.multiple_of(i * chunk + r * 32, 32), 32)
            normed[rows, :] = normalize(tok[rows, :].astype(F32), gain[...])

    tall = 512 if count % 512 == 0 else chunk

    def gated_piece(j, side):
        if j == 0:
            if side == 0:
                loads[1].wait()
                loads[2].wait()
            else:
                swaps[0].wait_recv()
                swaps[1].wait_recv()
        cols = slice(j * 128, (j + 1) * 128)
        to = slice(side * part + j * 128, side * part + (j + 1) * 128)

        @pl.loop(0, count // tall)
        def _(r):
            rows = pl.ds(pl.multiple_of(r * tall, tall), tall)
            hidden[rows, to] = gated_tile(normed[rows, :], lg[side, :, cols], lu[side, :, cols])

    stores = []
    wide = width // store_sem.shape[0]

    def down_piece(i):
        if i == 0:
            loads[6].wait()
            swaps[2].wait_recv()

        @pl.loop(0, (count // tall) * (wide // 256))
        def _(k):
            rows = pl.ds(pl.multiple_of(k % (count // tall) * tall, tall), tall)
            cols = pl.ds(pl.multiple_of(i * wide + k // (count // tall) * 256, 256), 256)
            out = jnp.dot(hidden[rows, :], ld[:, cols], preferred_element_type=F32)
            tok[rows, cols] = (tok[rows, cols].astype(F32) + out).astype(BF16)

        cols = pl.ds(i * wide, wide)
        copy = pltpu.make_async_copy(tok.at[:, cols], base_hbm.at[:, cols], store_sem.at[i])
        copy.start()
        stores.append(copy)

    before = [functools.partial(norm_piece, i) for i in range(count // chunk)]
    before += [functools.partial(gated_piece, j, 0) for j in range(part // 128)]
    after = [functools.partial(gated_piece, j, 1) for j in range(part // 128)]
    after += [functools.partial(down_piece, i) for i in range(store_sem.shape[0])]

    events = [plan.events(h) for h in range(2)]
    inners = [[e for e in events[h] if e[2] == 0] for h in range(2)]
    outers = [[e for e in events[h] if e[2]] for h in range(2)]

    steps = max(len(x) for x in inners)
    for s in range(max(steps, len(before))):
        if s < len(before):
            before[s]()
        for h in range(2):
            if s < len(inners[h]):
                arrive(h, inners[h][s])
                spread(h, inners[h][s])

    blocks = n * cap
    size = min(chunk, blocks)
    parts = blocks // size
    known = dims[1] <= 2 and dims[2] <= 2

    def part_of(h, e):
        if not known:
            return None
        rel = [0, 0, 0]
        for lvl, dim in enumerate(ORDERS[h]):
            rel[dim] = e[lvl]
        groups = dims[1] * dims[2]
        rank = (rel[1] * dims[2] + rel[2] + groups - 1) % groups
        return rank * dims[0] * cap // size

    def heavy_part(k):
        if k == 0:
            loads[3].wait()
            loads[4].wait()
            loads[5].wait()
        rows = pl.ds(k * size, size)
        gated(rows_in, rows, hg, hu, hhidden, pl.ds(0, size), 0)

        @pl.loop(0, width // 256)
        def _(j):
            cols = pl.ds(pl.multiple_of(j * 256, 256), 256)
            out = jnp.dot(hhidden[...], hd[:, cols], preferred_element_type=F32)
            rows_out[rows, cols] = out.astype(BF16)

    returns = []

    def collect(h, e):
        t = plan.token(h, e)
        rows, cols = rows_of(t), pl.ds(h * half, half)
        for _, cond, slot in plan.children(h, e):

            def take(slot=slot):
                view = back.at[h, slot]
                pltpu.make_async_copy(view, view, s_recv.at[h, slot]).wait()
                added = rows_out[rows, cols].astype(F32) + view[...].astype(F32)
                rows_out[rows, cols] = added.astype(BF16)

            when(cond, take)
        if plan.top(e) < 0:
            heavy_ref[:, cols] = rows_out[rows, cols]
            return
        to, slot = plan.parent(h, e)
        copy = pltpu.make_async_remote_copy(
            src_ref=rows_out.at[rows, cols],
            dst_ref=back.at[h, slot],
            send_sem=s_send.at[len(returns)],
            recv_sem=s_recv.at[h, slot],
            device_id={"light": plan.index(to)},
            device_id_type=MESH,
        )
        copy.start()
        returns.append(copy)

    arrived, returned = set(), set()
    for k in range(parts):
        for s in range(max(len(x) for x in outers)):
            for h in range(2):
                if s < len(outers[h]) and (h, outers[h][s]) not in arrived:
                    e = outers[h][s]
                    if part_of(h, e) in (None, k):
                        arrived.add((h, e))
                        arrive(h, e)
                        spread(h, e)
        heavy_part(k)
        if k == parts - 1 or known:
            for s in range(max(len(x) for x in outers)):
                for h in range(2):
                    if s < len(outers[h]):
                        e = outers[h][-1 - s]
                        if (h, e) not in returned and (k == parts - 1 or part_of(h, e) == k):
                            returned.add((h, e))
                            collect(h, e)

    for s in range(max(steps, len(after))):
        if s < len(after):
            after[s]()
        for h in range(2):
            if s < len(inners[h]):
                collect(h, inners[h][-1 - s])
    for h in range(2):
        collect(h, own)

    for copy, cond in sends:
        when(cond, copy.wait_send)
    for copy in returns:
        copy.wait_send()
    for copy in swaps:
        copy.wait_send()
    for copy in stores:
        copy.wait()


def place_kernel(base, heavy, idx, mask, out):
    rows, cap = base.shape[0], idx.shape[1]
    row_id = lax.broadcasted_iota(jnp.int32, (rows, cap), 0) + pl.program_id(0) * rows
    placing = jnp.where((row_id == idx[...]) & (mask[...] == 1), 1.0, 0.0).astype(BF16)
    added = jnp.dot(placing, heavy[...], preferred_element_type=F32)
    out[...] = (base[...].astype(F32) + added).astype(BF16)


def edge_counts(dims):
    plan = Plan(dims, 0)
    return [
        sum(len(plan.children(h, e)) for e in [(0, 0, 0)] + plan.events(h)) for h in range(2)
    ], plan.slots


def body(
    n,
    tokens,
    norm_gain,
    light_gate,
    light_up,
    light_down,
    heavy_gate,
    heavy_up,
    heavy_down,
    slot_token_index,
    slot_active_mask,
):
    count, width = tokens.shape
    cap = slot_token_index.shape[0]
    part, heavy = light_gate.shape[1], heavy_gate.shape[1]
    dims = three_factors(n)
    edges, slots = edge_counts(dims)
    blocks = n * cap
    hbm = pl.BlockSpec(memory_space=pl.ANY)
    vmem = pl.BlockSpec(memory_space=pltpu.VMEM)
    dma = pltpu.SemaphoreType.DMA
    base, rows = pl.pallas_call(
        functools.partial(routed_kernel, n, dims),
        out_shape=(
            jax.ShapeDtypeStruct((count, width), BF16),
            jax.ShapeDtypeStruct((cap, width), BF16),
        ),
        in_specs=[hbm, vmem] + [hbm] * 6 + [vmem] * 2,
        out_specs=(hbm, vmem),
        scratch_shapes=[
            pltpu.VMEM((count, width), BF16),
            pltpu.VMEM((count, width), BF16),
            pltpu.VMEM((2, width, part), BF16),
            pltpu.VMEM((2, width, part), BF16),
            pltpu.VMEM((2 * part, width), BF16),
            pltpu.VMEM((width, heavy), BF16),
            pltpu.VMEM((width, heavy), BF16),
            pltpu.VMEM((heavy, width), BF16),
            pltpu.VMEM((count, 2 * part), BF16),
            pltpu.VMEM((min(256, blocks), heavy), BF16),
            pltpu.VMEM((cap, width), F32),
            pltpu.VMEM((blocks, width), BF16),
            pltpu.VMEM((blocks, width), BF16),
            pltpu.VMEM((2, max(slots), cap, width // 2), BF16),
            dma((7,)),
            dma((3,)),
            dma((3,)),
            dma((width // 512,)),
            dma((sum(edges),)),
            dma((2, n)),
            dma((2 * (n - 1),)),
            dma((2, max(slots))),
        ],
        compiler_params=pltpu.CompilerParams(
            collective_id=0, has_side_effects=True, vmem_limit_bytes=62 * 2**20
        ),
    )(
        tokens,
        norm_gain.astype(F32)[None, :],
        light_gate,
        light_up,
        light_down,
        heavy_gate,
        heavy_up,
        heavy_down,
        slot_token_index[None, :],
        slot_active_mask[None, :],
    )
    tile = 256
    return pl.pallas_call(
        place_kernel,
        grid=(count // tile,),
        out_shape=jax.ShapeDtypeStruct((count, width), BF16),
        in_specs=[
            pl.BlockSpec((tile, width), lambda i: (i, 0)),
            pl.BlockSpec((cap, width), lambda i: (0, 0)),
            pl.BlockSpec((1, cap), lambda i: (0, 0)),
            pl.BlockSpec((1, cap), lambda i: (0, 0)),
        ],
        out_specs=pl.BlockSpec((tile, width), lambda i: (i, 0)),
    )(base, rows, slot_token_index[None, :], slot_active_mask[None, :])


def solution(mesh):
    placed = (
        P(("light", "pair"), None),
        P(),
        P(None, "pair"),
        P(None, "pair"),
        P("pair", None),
        P(None, "light"),
        P(None, "light"),
        P("light", None),
        P(("light", "pair")),
        P(("light", "pair")),
    )
    return jax.shard_map(
        functools.partial(body, mesh.shape["light"]),
        mesh=mesh,
        in_specs=placed,
        out_specs=P(("light", "pair"), None),
        check_vma=False,
    )
```

```python
import functools

import jax
import jax.numpy as jnp
from jax import lax
from jax.experimental import pallas as pl
from jax.experimental.pallas import tpu as pltpu
from jax.sharding import PartitionSpec as P

epsilon = 1e-06
MESH = pl.DeviceIdType.MESH
F32, BF16 = jnp.float32, jnp.bfloat16
ORDERS = ((0, 1, 2), (2, 0, 1))


def three_factors(n):
    dims, left = [], n
    for power in (3, 2, 1):
        f = 1
        while f**power < left or left % f:
            f += 1
        dims.append(f)
        left //= f
    return tuple(dims)


def kth_nearest(k, x, length):
    if k == 0:
        return x
    if length == 2:
        return 1 - x
    reach = jnp.minimum(x, length - 1 - x)
    sign = jnp.where(2 * x < length, 1, -1)
    both = k <= 2 * reach
    distance = jnp.where(both, (k + 1) // 2, k - reach)
    return x + distance * jnp.where(both, sign * (1 if k % 2 else -1), sign)


class Plan:
    def __init__(self, dims, me):
        self.dims = dims
        a, b, c = dims
        self.my = (me // (b * c), me // c % b, me % c)
        self.slots = []
        self.base = []
        for order in ORDERS:
            base, total, before = [], 0, 1
            for dim in order:
                base.append(total)
                length = dims[dim]
                total += before if length == 2 else before * (length + 1)
                before *= length
            self.base.append(base)
            self.slots.append(total)

    def events(self, h):
        a, p, q = (self.dims[d] for d in ORDERS[h])
        every = [(i, j, k) for i in range(a) for j in range(p) for k in range(q)]
        every.sort(key=lambda e: (e[2], e[0] + e[1], e[1]))
        return every[1:]

    def token(self, h, e):
        t = [None] * 3
        for lvl, dim in enumerate(ORDERS[h]):
            t[dim] = kth_nearest(e[lvl], self.my[dim], self.dims[dim])
        return tuple(t)

    def index(self, t):
        return (t[0] * self.dims[1] + t[1]) * self.dims[2] + t[2]

    def place(self, t, at):
        a, b, c = self.dims
        group = (t[1] - at[1] + b) % b * c + (t[2] - at[2] + c) % c
        return (group + b * c - 1) % (b * c) * a + t[0]

    def top(self, e):
        return max([-1] + [lvl for lvl in range(3) if e[lvl]])

    def moved(self, dim, x):
        at = list(self.my)
        at[dim] = x
        return tuple(at)

    def children(self, h, e):
        t, top, out = self.token(h, e), self.top(e), []
        for lvl in range(max(top, 0), 3):
            dim = ORDERS[h][lvl]
            length, x = self.dims[dim], self.my[dim]
            if length == 1:
                continue
            if lvl == top:
                if length > 2:
                    to = x + jnp.where(t[dim] < x, 1, -1)
                    cond = (to >= 0) & (to < length)
                    out.append((self.moved(dim, to), cond, self.slot(h, lvl, t, False)))
            elif length == 2:
                out.append((self.moved(dim, 1 - x), None, self.slot(h, lvl, t, False)))
            else:
                out.append((self.moved(dim, x + 1), x < length - 1, self.slot(h, lvl, t, False)))
                out.append((self.moved(dim, x - 1), x > 0, self.slot(h, lvl, t, True)))
        return out

    def slot(self, h, lvl, t, extra):
        order = ORDERS[h]
        prefix, before = 0, 1
        for dim in order[:lvl]:
            prefix = prefix * self.dims[dim] + t[dim]
            before *= self.dims[dim]
        length = self.dims[order[lvl]]
        base = self.base[h][lvl]
        if length == 2:
            return base + prefix
        main = base + prefix * length + t[order[lvl]]
        other = base + before * length + prefix
        if isinstance(extra, bool):
            return other if extra else main
        return jnp.where(extra, other, main)

    def parent(self, h, e):
        t, lvl = self.token(h, e), self.top(e)
        dim = ORDERS[h][lvl]
        x = self.my[dim]
        to = 1 - x if self.dims[dim] == 2 else x + jnp.where(t[dim] > x, 1, -1)
        extra = False if self.dims[dim] == 2 else (to == t[dim]) & (x < to)
        return self.moved(dim, to), self.slot(h, lvl, t, extra)


def first_columns(width):
    return width * 5 // 8 // 128 * 128


def when(cond, act):
    if cond is None:
        act()
    else:
        pl.when(cond)(act)


def normalize(rows, gain):
    square = jnp.mean(rows * rows, axis=-1, keepdims=True)
    return (rows * lax.rsqrt(square + epsilon) * gain).astype(BF16)


def gated_tile(x, gate, up):
    width = gate.shape[1]
    both = jnp.dot(x, jnp.concatenate([gate, up], axis=1), preferred_element_type=F32)
    g, u = both[:, :width], both[:, width:]
    return (g / (1.0 + jnp.exp(-g)) * u).astype(BF16)


def gated(x_ref, rows, gate_ref, up_ref, out_ref, out_rows, offset):
    width = gate_ref.shape[-1]
    if width % 128:
        x = x_ref[rows, :]
        g = jnp.dot(x, gate_ref[...], preferred_element_type=F32)
        u = jnp.dot(x, up_ref[...], preferred_element_type=F32)
        out_ref[out_rows, offset : offset + width] = (g / (1.0 + jnp.exp(-g)) * u).astype(BF16)
        return

    @pl.loop(0, width // 128)
    def _(j):
        cols = pl.ds(pl.multiple_of(j * 128, 128), 128)
        to = pl.ds(pl.multiple_of(offset + j * 128, 128), 128)
        out_ref[out_rows, to] = gated_tile(x_ref[rows, :], gate_ref[:, cols], up_ref[:, cols])


def routed_kernel(
    n, dims, *refs
):
    (tok_hbm, gain, lg_hbm, lu_hbm, ld_hbm, hg_hbm, hu_hbm, hd_hbm, idx, mask) = refs[:10]
    (base_hbm, heavy_ref) = refs[10:12]
    (tok, normed, lg, lu, ld, hg, hu, hd, hidden, hhidden, picked, rows_in, rows_out, back) = refs[12:26]
    (load_sem, pair_send, pair_recv, store_sem, g_send, g_recv, s_send, s_recv) = refs[26:]
    count, width = tok.shape
    cap = picked.shape[0]
    first = first_columns(width)
    columns = (pl.ds(0, first), pl.ds(first, width - first))
    part = lg.shape[2]
    me, core = lax.axis_index("light"), lax.axis_index("pair")
    plan = Plan(dims, me)
    chunk = 256

    loads = [
        pltpu.make_async_copy(s, d, load_sem.at[i])
        for i, (s, d) in enumerate(
            [
                (tok_hbm, tok),
                (lg_hbm, lg.at[0]),
                (lu_hbm, lu.at[0]),
                (hg_hbm, hg),
                (hu_hbm, hu),
                (hd_hbm, hd),
                (ld_hbm, ld.at[0:part]),
            ]
        )
    ]
    loads[0].start()

    barrier = pltpu.get_barrier_semaphore()
    neighbours = [({"pair": 1 - core}, None)]
    for dim, length in enumerate(dims):
        x = plan.my[dim]
        if length == 2:
            neighbours.append(({"light": plan.index(plan.moved(dim, 1 - x))}, None))
        elif length > 2:
            neighbours.append(({"light": plan.index(plan.moved(dim, x + 1))}, x < length - 1))
            neighbours.append(({"light": plan.index(plan.moved(dim, x - 1))}, x > 0))
    total = 0
    for device, cond in neighbours:
        when(
            cond,
            lambda device=device: pl.semaphore_signal(
                barrier, inc=1, device_id=device, device_id_type=MESH
            ),
        )
        total = total + (1 if cond is None else jnp.where(cond, 1, 0))
    pl.semaphore_wait(barrier, total)

    swaps = [
        pltpu.make_async_remote_copy(
            src_ref=s,
            dst_ref=d,
            send_sem=pair_send.at[i],
            recv_sem=pair_recv.at[i],
            device_id={"pair": 1 - core},
            device_id_type=MESH,
        )
        for i, (s, d) in enumerate(
            [(lg_hbm, lg.at[1]), (lu_hbm, lu.at[1]), (ld_hbm, ld.at[part : 2 * part])]
        )
    ]

    loads[0].wait()
    for copy in loads[1:]:
        copy.start()

    live = jnp.where(mask[...] == 1, idx[...], -1).astype(F32)
    diagonal = lax.broadcasted_iota(jnp.int32, (cap, cap), 0) == lax.broadcasted_iota(
        jnp.int32, (cap, cap), 1
    )
    wanted = jnp.sum(jnp.where(diagonal, live, 0.0), axis=1, keepdims=True)
    row_id = lax.broadcasted_iota(jnp.int32, (cap, count), 1).astype(F32)
    taking = jnp.where(row_id == wanted, 1.0, 0.0).astype(BF16)
    for j in range(width // 512):
        cols = slice(j * 512, (j + 1) * 512)
        picked[:, cols] = jnp.dot(taking, tok[:, cols], preferred_element_type=F32)

    def rows_of(t):
        return pl.ds(pl.multiple_of(plan.place(t, plan.my) * cap, cap), cap)

    mine = rows_of(plan.my)
    rows_in[mine, :] = normalize(picked[...], gain[...])

    sends = []

    def spread(h, e):
        t = plan.token(h, e)
        cols = columns[h]
        for to, cond, _ in plan.children(h, e):
            target = pl.ds(pl.multiple_of(plan.place(t, to) * cap, cap), cap)
            copy = pltpu.make_async_remote_copy(
                src_ref=rows_in.at[rows_of(t), cols],
                dst_ref=rows_in.at[target, cols],
                send_sem=g_send.at[len(sends)],
                recv_sem=g_recv.at[h, plan.index(t)],
                device_id={"light": plan.index(to)},
                device_id_type=MESH,
            )
            when(cond, copy.start)
            sends.append((copy, cond))

    def arrive(h, e):
        t = plan.token(h, e)
        view = rows_in.at[rows_of(t), columns[h]]
        pltpu.make_async_copy(view, view, g_recv.at[h, plan.index(t)]).wait()

    own = (0, 0, 0)
    for h in range(2):
        spread(h, own)
    for copy in swaps:
        copy.start()

    def norm_piece(i):
        @pl.loop(0, chunk // 32)
        def _(r):
            rows = pl.ds(pl.multiple_of(i * chunk + r * 32, 32), 32)
            normed[rows, :] = normalize(tok[rows, :].astype(F32), gain[...])

    tall = 512 if count % 512 == 0 else chunk

    def gated_piece(j, side):
        if j == 0:
            if side == 0:
                loads[1].wait()
                loads[2].wait()
            else:
                swaps[0].wait_recv()
                swaps[1].wait_recv()
        cols = slice(j * 128, (j + 1) * 128)
        to = slice(side * part + j * 128, side * part + (j + 1) * 128)

        @pl.loop(0, count // tall)
        def _(r):
            rows = pl.ds(pl.multiple_of(r * tall, tall), tall)
            hidden[rows, to] = gated_tile(normed[rows, :], lg[side, :, cols], lu[side, :, cols])

    stores = []
    wide = width // store_sem.shape[0]

    def down_piece(i):
        if i == 0:
            loads[6].wait()
            swaps[2].wait_recv()

        @pl.loop(0, (count // tall) * (wide // 256))
        def _(k):
            rows = pl.ds(pl.multiple_of(k % (count // tall) * tall, tall), tall)
            cols = pl.ds(pl.multiple_of(i * wide + k // (count // tall) * 256, 256), 256)
            out = jnp.dot(hidden[rows, :], ld[:, cols], preferred_element_type=F32)
            tok[rows, cols] = (tok[rows, cols].astype(F32) + out).astype(BF16)

        cols = pl.ds(i * wide, wide)
        copy = pltpu.make_async_copy(tok.at[:, cols], base_hbm.at[:, cols], store_sem.at[i])
        copy.start()
        stores.append(copy)

    before = [functools.partial(norm_piece, i) for i in range(count // chunk)]
    before += [functools.partial(gated_piece, j, 0) for j in range(part // 128)]
    after = [functools.partial(gated_piece, j, 1) for j in range(part // 128)]
    after += [functools.partial(down_piece, i) for i in range(store_sem.shape[0])]

    events = [plan.events(h) for h in range(2)]
    inners = [[e for e in events[h] if e[2] == 0] for h in range(2)]
    outers = [[e for e in events[h] if e[2]] for h in range(2)]

    steps = max(len(x) for x in inners)
    for s in range(max(steps, len(before))):
        if s < len(before):
            before[s]()
        for h in range(2):
            if s < len(inners[h]):
                arrive(h, inners[h][s])
                spread(h, inners[h][s])

    blocks = n * cap
    size = min(chunk, blocks)
    parts = blocks // size
    known = dims[1] <= 2 and dims[2] <= 2

    def part_of(h, e):
        if not known:
            return None
        rel = [0, 0, 0]
        for lvl, dim in enumerate(ORDERS[h]):
            rel[dim] = e[lvl]
        groups = dims[1] * dims[2]
        rank = (rel[1] * dims[2] + rel[2] + groups - 1) % groups
        return rank * dims[0] * cap // size

    def heavy_part(k):
        if k == 0:
            loads[3].wait()
            loads[4].wait()
            loads[5].wait()
        rows = pl.ds(k * size, size)
        gated(rows_in, rows, hg, hu, hhidden, pl.ds(0, size), 0)

        @pl.loop(0, width // 256)
        def _(j):
            cols = pl.ds(pl.multiple_of(j * 256, 256), 256)
            out = jnp.dot(hhidden[...], hd[:, cols], preferred_element_type=F32)
            rows_out[rows, cols] = out.astype(BF16)

    returns = []

    def collect(h, e):
        t = plan.token(h, e)
        rows, cols = rows_of(t), columns[h]
        for _, cond, slot in plan.children(h, e):

            def take(slot=slot):
                view = back.at[h, slot, :, pl.ds(0, cols.size)]
                pltpu.make_async_copy(view, view, s_recv.at[h, slot]).wait()
                added = rows_out[rows, cols].astype(F32) + view[...].astype(F32)
                rows_out[rows, cols] = added.astype(BF16)

            when(cond, take)
        if plan.top(e) < 0:
            heavy_ref[:, cols] = rows_out[rows, cols]
            return
        to, slot = plan.parent(h, e)
        copy = pltpu.make_async_remote_copy(
            src_ref=rows_out.at[rows, cols],
            dst_ref=back.at[h, slot, :, pl.ds(0, cols.size)],
            send_sem=s_send.at[len(returns)],
            recv_sem=s_recv.at[h, slot],
            device_id={"light": plan.index(to)},
            device_id_type=MESH,
        )
        copy.start()
        returns.append(copy)

    arrived, returned = set(), set()
    for k in range(parts):
        for s in range(max(len(x) for x in outers)):
            for h in range(2):
                if s < len(outers[h]) and (h, outers[h][s]) not in arrived:
                    e = outers[h][s]
                    if part_of(h, e) in (None, k):
                        arrived.add((h, e))
                        arrive(h, e)
                        spread(h, e)
        heavy_part(k)
        if k == parts - 1 or known:
            for s in range(max(len(x) for x in outers)):
                for h in range(2):
                    if s < len(outers[h]):
                        e = outers[h][-1 - s]
                        if (h, e) not in returned and (k == parts - 1 or part_of(h, e) == k):
                            returned.add((h, e))
                            collect(h, e)

    for s in range(max(steps, len(after))):
        if s < len(after):
            after[s]()
        for h in range(2):
            if s < len(inners[h]):
                collect(h, inners[h][-1 - s])
    for h in range(2):
        collect(h, own)

    for copy, cond in sends:
        when(cond, copy.wait_send)
    for copy in returns:
        copy.wait_send()
    for copy in swaps:
        copy.wait_send()
    for copy in stores:
        copy.wait()


def place_kernel(base, heavy, idx, mask, out):
    rows, cap = base.shape[0], idx.shape[1]
    row_id = lax.broadcasted_iota(jnp.int32, (rows, cap), 0) + pl.program_id(0) * rows
    placing = jnp.where((row_id == idx[...]) & (mask[...] == 1), 1.0, 0.0).astype(BF16)
    added = jnp.dot(placing, heavy[...], preferred_element_type=F32)
    out[...] = (base[...].astype(F32) + added).astype(BF16)


def edge_counts(dims):
    plan = Plan(dims, 0)
    return [
        sum(len(plan.children(h, e)) for e in [(0, 0, 0)] + plan.events(h)) for h in range(2)
    ], plan.slots


def body(
    n,
    tokens,
    norm_gain,
    light_gate,
    light_up,
    light_down,
    heavy_gate,
    heavy_up,
    heavy_down,
    slot_token_index,
    slot_active_mask,
):
    count, width = tokens.shape
    cap = slot_token_index.shape[0]
    part, heavy = light_gate.shape[1], heavy_gate.shape[1]
    dims = three_factors(n)
    edges, slots = edge_counts(dims)
    blocks = n * cap
    hbm = pl.BlockSpec(memory_space=pl.ANY)
    vmem = pl.BlockSpec(memory_space=pltpu.VMEM)
    dma = pltpu.SemaphoreType.DMA
    base, rows = pl.pallas_call(
        functools.partial(routed_kernel, n, dims),
        out_shape=(
            jax.ShapeDtypeStruct((count, width), BF16),
            jax.ShapeDtypeStruct((cap, width), BF16),
        ),
        in_specs=[hbm, vmem] + [hbm] * 6 + [vmem] * 2,
        out_specs=(hbm, vmem),
        scratch_shapes=[
            pltpu.VMEM((count, width), BF16),
            pltpu.VMEM((count, width), BF16),
            pltpu.VMEM((2, width, part), BF16),
            pltpu.VMEM((2, width, part), BF16),
            pltpu.VMEM((2 * part, width), BF16),
            pltpu.VMEM((width, heavy), BF16),
            pltpu.VMEM((width, heavy), BF16),
            pltpu.VMEM((heavy, width), BF16),
            pltpu.VMEM((count, 2 * part), BF16),
            pltpu.VMEM((min(256, blocks), heavy), BF16),
            pltpu.VMEM((cap, width), F32),
            pltpu.VMEM((blocks, width), BF16),
            pltpu.VMEM((blocks, width), BF16),
            pltpu.VMEM((2, max(slots), cap, first_columns(width)), BF16),
            dma((7,)),
            dma((3,)),
            dma((3,)),
            dma((width // 512,)),
            dma((sum(edges),)),
            dma((2, n)),
            dma((2 * (n - 1),)),
            dma((2, max(slots))),
        ],
        compiler_params=pltpu.CompilerParams(
            collective_id=0, has_side_effects=True, vmem_limit_bytes=62 * 2**20
        ),
    )(
        tokens,
        norm_gain.astype(F32)[None, :],
        light_gate,
        light_up,
        light_down,
        heavy_gate,
        heavy_up,
        heavy_down,
        slot_token_index[None, :],
        slot_active_mask[None, :],
    )
    tile = 256
    return pl.pallas_call(
        place_kernel,
        grid=(count // tile,),
        out_shape=jax.ShapeDtypeStruct((count, width), BF16),
        in_specs=[
            pl.BlockSpec((tile, width), lambda i: (i, 0)),
            pl.BlockSpec((cap, width), lambda i: (0, 0)),
            pl.BlockSpec((1, cap), lambda i: (0, 0)),
            pl.BlockSpec((1, cap), lambda i: (0, 0)),
        ],
        out_specs=pl.BlockSpec((tile, width), lambda i: (i, 0)),
    )(base, rows, slot_token_index[None, :], slot_active_mask[None, :])


def solution(mesh):
    placed = (
        P(("light", "pair"), None),
        P(),
        P(None, "pair"),
        P(None, "pair"),
        P("pair", None),
        P(None, "light"),
        P(None, "light"),
        P("light", None),
        P(("light", "pair")),
        P(("light", "pair")),
    )
    return jax.shard_map(
        functools.partial(body, mesh.shape["light"]),
        mesh=mesh,
        in_specs=placed,
        out_specs=P(("light", "pair"), None),
        check_vma=False,
    )
```
